32 devices in a mesh: wa: 2 (over x), uv: 16 (over z, y, core).
Axes of the slice: x: 2, y: 2, z: 4, core: 2. Of those that a mesh axis runs over, the one named last changes fastest.
Arguments:
- visibility: bfloat16 [1536, 2, 256], P(('wa', 'uv')), may hold values from -6 to 6
- coords: bfloat16 [1536, 2, 256], P(('wa', 'uv')), may hold values from -24 to 24
- tile_row: int32 [1536, 1], P(('wa', 'uv')), may hold values from 0 to 63; in each aligned block of 48 rows (0 to 47, 48 to 95, ...) at most 2 rows name the same one
- col_offset: int32 [1536], P(('wa', 'uv')), may hold values from 0 to 4032
- live_count: int32 [2, 16], P('wa', 'uv'), may hold values from 1 to 48, 480 in all within a row
Outputs:
- sky_image: float32 [4096, 4096], P('uv', 'wa')
The draws below stay inside these ranges and needn't reach their ends.
Inputs may be any that keep to these rules, and one draw needn't show every extreme that they name: `tile_row`: within the blocks of one device, at most 2 name the same tile row, and some device reaches 2. A device's live blocks are its first live_count ones; in each w group the 16 counts sum to 480, and the largest count is 48.
All inputs are finite; a program needn't handle non-finite values.
Results may differ from the reference program's by a relative error of at most 0.0069.
Values may be sent and summed in bfloat16 or wider, within the bound.
A program may use at most 128 MiB of HBM per device.

```python
import math
import jax
import jax.numpy as jnp
import numpy as np
from jax import lax

G = 4096
SUB = 64
B_DEV = 48
CAP = 2
K = 256
BLOCKS = 1536
N_WA = 2
N_UV = 16


def plant(array, rng, low, top_value):
    shape = array.shape
    index_at = [jax.random.randint(jax.random.fold_in(rng, axis), (), 0, shape[axis]) for axis in range(len(shape))]
    array = array.at[tuple(index_at)].set(low)
    longest = shape.index(max(shape))
    index_at[longest] = (index_at[longest] + 1) % shape[longest]
    return array.at[tuple(index_at)].set(top_value)


def shard_levels(stream_key, dims, split, least, largest):
    level = 1.0
    for dim, parts in split:
        heights = jax.random.uniform(jax.random.fold_in(jax.random.fold_in(stream_key, 6), dim), (parts,), jnp.float32, least / len(split), largest / len(split))
        level = level * jnp.repeat(jnp.exp(heights), dims[dim] // parts).reshape((-1,) + (1,) * (len(dims) - 1 - dim))
    return level


def length_profile(number_of, total, reach, slope):
    portions = [(1 << 20) // math.isqrt(standing ** slope) + 1 for standing in range(2, number_of + 1)]
    rest, holding = total - reach - (number_of - 1), [1] * (number_of - 1)
    while rest > 0:
        free = [i for i in range(number_of - 1) if holding[i] < reach]
        whole, left = sum([portions[i] for i in free]), rest
        for i in free:
            extra = min(reach - holding[i], max(1, left * portions[i] // whole), rest)
            holding[i] = holding[i] + extra
            rest = rest - extra
    return np.array([reach] + holding)


def uneven(stream_key, count, total, bound, skew):
    if count == 2:
        one = jax.random.randint(stream_key, (), max(1, total - bound), min(bound, total - 1) + 1)
        return jnp.stack([one, total - one])
    sizes = jnp.asarray(length_profile(count, total, bound, skew), jnp.int32)
    couples = (count - 1) // 2
    giver, sink = sizes[1:1 + 2 * couples:2], sizes[2:2 + 2 * couples:2]
    slack = jnp.minimum(giver - 1, bound - sink)
    shifted = jax.random.randint(jax.random.fold_in(stream_key, 1), (couples,), 0, 1 << 20) % (slack + 1)
    sizes = sizes.at[1:1 + 2 * couples:2].set(giver - shifted).at[2:2 + 2 * couples:2].set(sink + shifted)
    return sizes[jax.random.permutation(jax.random.fold_in(stream_key, 2), count)]


def deal_out(stream_key, own, number, rows, count, top, most, lean):
    sequence = jax.random.permutation(stream_key, count)
    heavy_load, ordinary = shares(count, rows * top, most, lean, True), shares(count, rows * top, most, lean, False)
    places = jnp.arange(count)

    def named(sizes, offset_by):
        used = int((sizes > 0).sum())
        fixed = max(1, used // 4)
        shifted = fixed + (places - fixed + offset_by * (used - fixed)) % max(1, count - fixed)
        return jnp.zeros((count,), jnp.int32).at[sequence[jnp.where(places < fixed, places, shifted)]].set(jnp.asarray(sizes, jnp.int32))

    sizes = jnp.where(number % 4 == 0, named(heavy_load, number // 4), named(ordinary, number - number // 4 - 1))
    mixed = jax.random.permutation(jax.random.fold_in(own, 3), count)
    donor, receiver = mixed[0:count // 2 * 2:2], mixed[1:count // 2 * 2:2]
    margin = jnp.minimum(sizes[donor] - 1, most - sizes[receiver]) // 2
    margin = jnp.where((donor == sequence[0]) | (receiver == sequence[0]) | (sizes[receiver] == 0), 0, jnp.maximum(margin, 0))
    shifted = jax.random.randint(jax.random.fold_in(own, 4), (count // 2,), 0, 1 << 20) % (margin + 1)
    sizes = sizes.at[donor].add(-shifted).at[receiver].add(shifted)
    members = jnp.searchsorted(jnp.cumsum(sizes), jnp.arange(rows * top), side="right").astype(jnp.int32)
    listing = members.reshape(top, rows).T
    listing = listing[jax.random.permutation(jax.random.fold_in(own, 1), rows)]
    offset_by = jax.random.randint(jax.random.fold_in(own, 2), (rows, 1), 0, top)
    return jnp.take_along_axis(listing, (jnp.arange(top)[None, :] + offset_by) % top, axis=1)


def shares(number_of, total, reach, slope, full):
    weights = [(1 << 20) // math.isqrt(standing ** slope) + 1 for standing in range(1, number_of + 1)]
    largest = reach if full else min(reach, max(-(-total // number_of), total * weights[0] // sum(weights)))
    least = 1 if total - largest >= number_of - 1 else 0
    counts, rest = [largest] + [least] * (number_of - 1), total - largest - least * (number_of - 1)
    while rest > 0:
        movable = [i for i in range(1, number_of) if counts[i] < largest] or [i for i in range(1, number_of) if counts[i] < reach]
        mass, budget = sum([weights[i] for i in movable]), rest
        for i in movable:
            more = min(reach - counts[i], max(1, budget * weights[i] // mass), rest)
            counts[i] = counts[i] + more
            rest = rest - more
    return np.array(counts)


def centred(key, dims, spread, reach, pieces=(), dtype=jnp.bfloat16):
    drawn = spread * jax.random.normal(key, dims, jnp.float32)
    if pieces:
        drawn = drawn * shard_levels(key, dims, pieces, -0.22, 0.18)
    return jnp.clip(drawn, -reach, reach).astype(dtype)


def setup_inputs(seed: int = 0) -> dict:
    keys = jax.random.split(jax.random.key(seed), 6)
    visibility = centred(keys[0], (BLOCKS, 2, K), 1.0, 6.0, ((0, 32),))
    coords = jnp.clip(jax.random.uniform(keys[1], (BLOCKS, 2, K), jnp.float32, -24.0, 24.0) * shard_levels(keys[1], (BLOCKS, 2, K), ((0, 32),), -0.4, 0.0), -24.0, 24.0).astype(jnp.bfloat16)
    tile_row_keys = jax.random.split(jax.random.fold_in(keys[2], 1), BLOCKS // B_DEV)
    tile_row_turns = jax.random.permutation(jax.random.fold_in(keys[2], 3), BLOCKS // B_DEV)
    tile_row = jax.vmap(lambda own, number: deal_out(jax.random.fold_in(keys[2], 2), own, number, B_DEV, G // SUB, 1, CAP, 2))(tile_row_keys, tile_row_turns).reshape((BLOCKS, 1))
    col_offset = plant(jax.random.randint(keys[3], (BLOCKS,), 0, G - SUB + 1), jax.random.fold_in(keys[3], 1), 0, G - SUB).astype(jnp.int32)
    live_count = jax.vmap(lambda own: uneven(own, N_UV, 5 * B_DEV * N_UV // 8, B_DEV, 2))(jax.random.split(keys[4], N_WA)).reshape((N_WA, N_UV)).astype(jnp.int32)
    return {"visibility": visibility, "coords": coords, "tile_row": tile_row, "col_offset": col_offset, "live_count": live_count}


full_turn = 2.0 * math.pi
plane_step = 6.0

def centered(length):
    return (jnp.arange(length) - length // 2).astype(jnp.float32)

def subgrid_angles(coord_col, side_len):
    return full_turn / side_len * (centered(side_len)[None, :, None] * coord_col[:, None, :])

def fourier_pair(side_len):
    offsets = (jnp.arange(side_len) - side_len // 2).astype(jnp.int32)
    product = jnp.mod(offsets[:, None] * offsets[None, :], side_len)
    angles = full_turn / side_len * product.astype(jnp.float32)
    return (jnp.cos(angles), -jnp.sin(angles))

def multiply(einsum_form, first, second):
    return jnp.einsum(einsum_form, first.astype(jnp.float32), second.astype(jnp.float32), precision=lax.Precision.HIGHEST)

def make_subgrids(samples, coords):
    norm_scale = 1.0 / math.sqrt(samples.shape[2])
    angle_u = subgrid_angles(coords[:, 0, :].astype(jnp.float32), SUB)
    angle_v = subgrid_angles(coords[:, 1, :].astype(jnp.float32), SUB)
    cos_u, sin_u = (jnp.cos(angle_u), jnp.sin(angle_u))
    vis_re = samples[:, 0, :].astype(jnp.float32)[:, None, :]
    vis_im = samples[:, 1, :].astype(jnp.float32)[:, None, :]
    left_re = ((vis_re * cos_u - vis_im * sin_u) * norm_scale).astype(jnp.bfloat16)
    left_im = ((vis_re * sin_u + vis_im * cos_u) * norm_scale).astype(jnp.bfloat16)
    right_re = jnp.cos(angle_v).astype(jnp.bfloat16)
    right_im = jnp.sin(angle_v).astype(jnp.bfloat16)
    form_s = 'nlk,nmk->nlm'
    sub_re = (multiply(form_s, left_re, right_re) - multiply(form_s, left_im, right_im)).astype(jnp.bfloat16)
    sub_im = (multiply(form_s, left_re, right_im) + multiply(form_s, left_im, right_re)).astype(jnp.bfloat16)
    four_re, four_im = fourier_pair(SUB)
    four_re = four_re.astype(jnp.bfloat16)
    four_im = four_im.astype(jnp.bfloat16)
    form_a = 'pl,nlm->npm'
    temp_re = (multiply(form_a, four_re, sub_re) - multiply(form_a, four_im, sub_im)).astype(jnp.bfloat16)
    temp_im = (multiply(form_a, four_re, sub_im) + multiply(form_a, four_im, sub_re)).astype(jnp.bfloat16)
    form_b = 'npm,qm->npq'
    out_re = multiply(form_b, temp_re, four_re) - multiply(form_b, temp_im, four_im)
    out_im = multiply(form_b, temp_re, four_im) + multiply(form_b, temp_im, four_re)
    return (jnp.stack([out_re, out_im], axis=1) * (1.0 / SUB)).astype(jnp.bfloat16)

def reference(visibility, coords, tile_row, col_offset, live_count):
    vis_groups = visibility.reshape(N_WA, N_UV, B_DEV, 2, K)
    coord_groups = coords.reshape(N_WA, N_UV, B_DEV, 2, K)
    tile_groups = tile_row.reshape(N_WA, N_UV, B_DEV).astype(jnp.int32)
    col_groups = col_offset.reshape(N_WA, N_UV, B_DEV).astype(jnp.int32)
    checker = (1 - 2 * (jnp.arange(G) % 2)).astype(jnp.float32)
    checker_grid = checker[:, None] * checker[None, :]
    axis_coord = centered(G) / G
    depth_term = jnp.sqrt(1.0 - axis_coord[:, None] ** 2 - axis_coord[None, :] ** 2)
    offsets = jnp.arange(SUB).astype(jnp.int32)

    def per_device(pair_args):
        return make_subgrids(pair_args[0], pair_args[1])

    def fold_group(accumulated, group_args):
        vis_g, coord_g, tile_g, col_g, count_g, group_index = group_args
        built = lax.map(per_device, (vis_g, coord_g))
        live_mask = jnp.arange(B_DEV).astype(jnp.int32)[None, :] < count_g[:, None]
        row_index = tile_g[:, :, None, None] * SUB + offsets[None, None, :, None]
        row_index = jnp.broadcast_to(row_index, (N_UV, B_DEV, SUB, SUB))
        col_index = jnp.broadcast_to(col_g[:, :, None, None] + offsets[None, None, None, :], (N_UV, B_DEV, SUB, SUB))
        row_index = jnp.where(live_mask[:, :, None, None], row_index, G)
        values = jnp.moveaxis(built.astype(jnp.float32), 2, 0)
        plane_grid = jnp.zeros((2, G, G), jnp.float32).at[:, row_index, col_index].add(values, mode='drop')
        spectrum = (plane_grid[0] + 1j * plane_grid[1]) * checker_grid
        plane_image = (jnp.fft.ifft2(spectrum) * G * checker_grid).T
        plane_depth = (group_index.astype(jnp.float32) - (N_WA - 1) / 2.0) * plane_step
        screen_angle = full_turn * plane_depth * (depth_term - 1.0)
        term = jnp.real(plane_image) * jnp.cos(screen_angle) - jnp.imag(plane_image) * jnp.sin(screen_angle)
        return (accumulated + term.astype(jnp.float32), None)
    summed, _ = lax.scan(fold_group, jnp.zeros((G, G), jnp.float32), (vis_groups, coord_groups, tile_groups, col_groups, live_count.astype(jnp.int32), jnp.arange(N_WA).astype(jnp.int32)))
    return summed
```

```python
import functools
import math

import jax
import jax.numpy as jnp
import ml_dtypes
import numpy as np
from jax import lax
from jax.experimental import pallas as pl
from jax.experimental.pallas import tpu as pltpu
from jax.sharding import PartitionSpec as P

G = 4096
SUB = 64
UNROLL = 4
plane_step = 6.0
full_turn = 2.0 * math.pi
BF = ml_dtypes.bfloat16


def turn_poly():
    nodes = np.cos(np.pi * (np.arange(256) + 0.5) / 256)
    z = (nodes + 1.0) / 8.0
    f = np.sqrt(z)
    cos_c = np.polynomial.chebyshev.cheb2poly(
        np.polynomial.chebyshev.chebfit(nodes, np.cos(2 * np.pi * f), 7)
    )
    sin_c = np.polynomial.chebyshev.cheb2poly(
        np.polynomial.chebyshev.chebfit(nodes, np.sin(2 * np.pi * f) / f, 7)
    )
    base = np.polynomial.Polynomial([-1.0, 8.0])
    out = []
    for coefs in (cos_c, sin_c):
        total = np.polynomial.Polynomial([0.0])
        for c in coefs[::-1]:
            total = total * base + c
        out.append([float(c) for c in total.coef])
    return out


COS_C, SIN_C = turn_poly()


def cos_sin_turns(turns):
    f = turns - jnp.round(turns)
    z = f * f
    c = jnp.full_like(z, COS_C[-1])
    for k in COS_C[-2::-1]:
        c = c * z + k
    s = jnp.full_like(z, SIN_C[-1])
    for k in SIN_C[-2::-1]:
        s = s * z + k
    return c, s * f


def factor_table():
    o = np.arange(SUB) - SUB // 2
    ang = full_turn / SUB * np.mod(o[:, None] * o[None, :], SUB)
    return np.cos(ang).astype(BF), (-np.sin(ang)).astype(BF)


def factor_matrix():
    fr, fi = factor_table()
    return np.block([[fr, -fi], [fi, fr]]).astype(BF)


def head_matrix():
    k = np.arange(64)
    ang = full_turn / 64 * np.mod(k[:, None] * k[None, :], 64)
    c, s = np.cos(ang), np.sin(ang)
    return np.block([[c, -s], [s, c]]).astype(BF)


def tail_matrices():
    l0 = np.arange(64)[:, None, None]
    p = np.arange(64)[None, :, None]
    l1 = np.arange(64)[None, None, :]
    ang = full_turn / G * np.mod(p * (l0 + 64 * l1), G)
    sign = 1.0 - 2.0 * ((p + l0) % 2)
    c, s = np.cos(ang) * sign, np.sin(ang) * sign
    top = np.concatenate([c, s], axis=2)
    bottom = np.concatenate([-s, c], axis=2)
    return np.concatenate([top, bottom], axis=1).astype(BF)


def grid_kernel(width, tiles, counts, data_ref, phase_ref, mf_ref, d_ref, out_ref, acc):
    j = pl.program_id(0)
    blocks = data_ref.shape[0]

    @pl.when(j == 0)
    def _():
        acc[...] = jnp.zeros_like(acc)

    total = counts[j]
    offs = lax.broadcasted_iota(jnp.int32, (8, data_ref.shape[2]), 0).astype(jnp.float32)
    fine = offs * (1.0 / SUB)
    coarse = (offs - 4.0) * (8.0 / SUB)
    scale = 1.0 / math.sqrt(data_ref.shape[2])

    def expand(pr, pi, c1, s1):
        res, ims = [], []
        for a in range(8):
            ar, ai = pr[a : a + 1, :], pi[a : a + 1, :]
            res.append(ar * c1 - ai * s1)
            ims.append(ar * s1 + ai * c1)
        return jnp.concatenate(res + ims, axis=0).astype(jnp.bfloat16)

    def step(it, carry):
        lefts, rights = [], []
        for k in range(UNROLL):
            i = it * UNROLL + k
            keep = jnp.where(i < total, scale, 0.0)
            row = data_ref[i]
            vr, vi, u, v = (row[n : n + 1, :] for n in range(4))
            c1, s1 = cos_sin_turns(fine * u)
            c8, s8 = cos_sin_turns(coarse * u)
            lefts.append(
                expand((vr * c8 - vi * s8) * keep, (vr * s8 + vi * c8) * keep, c1, s1)
            )
            d1, t1 = cos_sin_turns(fine * v)
            d8, t8 = cos_sin_turns(coarse * v)
            rights.append(expand(d8, t8, d1, t1))
        parts = []
        for k in range(UNROLL):
            s = lax.dot_general(
                lefts[k], rights[k], (((1,), (1,)), ((), ())), preferred_element_type=jnp.float32
            ).astype(jnp.bfloat16)
            c = jnp.dot(mf_ref[...], s, preferred_element_type=jnp.float32).astype(jnp.bfloat16)
            parts.append(jnp.concatenate([c[:SUB], c[SUB:]], axis=1))
        h = jnp.dot(jnp.concatenate(parts, axis=0), d_ref[...], preferred_element_type=jnp.float32)
        for k in range(UNROLL):
            i = it * UNROLL + k
            ph = phase_ref[i]
            pr, pi = ph[0:1, :], ph[1:2, :]
            hr = h[k * SUB : (k + 1) * SUB, :width]
            hi = h[k * SUB : (k + 1) * SUB, width:]
            rows = pl.ds(pl.multiple_of(tiles[j * blocks + i] * SUB, SUB), SUB)
            acc[0, rows, :] += hr * pr - hi * pi
            acc[1, rows, :] += hr * pi + hi * pr
        return carry

    lax.fori_loop(0, (total + UNROLL - 1) // UNROLL, step, 0)

    @pl.when(j == pl.num_programs(0) - 1)
    def _():
        out_ref[...] = acc[...].astype(jnp.bfloat16)


def on_device(visibility, coords, tile_row, col_offset, live_count):
    uv_count = lax.axis_size("uv")
    wa_count = lax.axis_size("wa")
    uv_index = lax.axis_index("uv")
    wa_index = lax.axis_index("wa")
    blocks = visibility.shape[0]
    k_len = visibility.shape[2]
    width = G // uv_count
    placement = jnp.concatenate(
        [tile_row[:, 0], col_offset, jnp.broadcast_to(live_count[0], (blocks,))]
    )
    all_place = lax.all_gather(placement, "uv", axis=0).reshape(uv_count, 3, blocks)
    tiles = all_place[:, 0].reshape(-1)
    cols = all_place[:, 1].reshape(-1)
    counts = all_place[:, 2, 0]
    data = jnp.concatenate([visibility, coords], axis=1)
    all_data = lax.all_gather(data, "uv", axis=0, tiled=True).astype(jnp.float32)

    m_off = uv_index * width + jnp.arange(width) - G // 2
    turn = jnp.mod((cols[:, None] - G // 2) * m_off[None, :], G).astype(jnp.float32) * (1.0 / G)
    pc, ps = cos_sin_turns(turn)
    phase = jnp.stack([pc, ps], axis=1)

    fr, fi = factor_table()
    fr, fi = jnp.asarray(fr.astype(np.float32)), jnp.asarray(fi.astype(np.float32))
    qt = jnp.mod(jnp.arange(SUB)[:, None] * m_off[None, :], G).astype(jnp.float32) * (1.0 / G)
    qc, qs = cos_sin_turns(qt)
    mm = functools.partial(jnp.einsum, "qk,qm->km", precision=lax.Precision.HIGHEST)
    dr = (mm(fr, qc) - mm(fi, qs)) * (1.0 / SUB)
    di = (mm(fr, qs) + mm(fi, qc)) * (1.0 / SUB)
    ddr = jnp.concatenate([dr, -di], axis=0)
    ddi = jnp.concatenate([di, dr], axis=0)
    d_table = jnp.concatenate(
        [jnp.concatenate([ddr, ddi], axis=1), jnp.concatenate([-ddi, ddr], axis=1)], axis=0
    ).astype(jnp.bfloat16)

    spec = pltpu.PrefetchScalarGridSpec(
        num_scalar_prefetch=2,
        grid=(uv_count,),
        in_specs=[
            pl.BlockSpec((blocks, 4, k_len), lambda j, *_: (j, 0, 0)),
            pl.BlockSpec((blocks, 2, width), lambda j, *_: (j, 0, 0)),
            pl.BlockSpec((2 * SUB, 2 * SUB), lambda j, *_: (0, 0)),
            pl.BlockSpec((4 * SUB, 2 * width), lambda j, *_: (0, 0)),
        ],
        out_specs=pl.BlockSpec((2, G, width), lambda j, *_: (0, 0, 0)),
        scratch_shapes=[pltpu.VMEM((2, G, width), jnp.float32)],
    )
    half = pl.pallas_call(
        functools.partial(grid_kernel, width),
        out_shape=jax.ShapeDtypeStruct((2, G, width), jnp.bfloat16),
        grid_spec=spec,
        compiler_params=pltpu.CompilerParams(vmem_limit_bytes=40 * 1024 * 1024),
    )(tiles, counts, all_data, phase, jnp.asarray(factor_matrix()), d_table)

    first = jnp.dot(
        jnp.asarray(head_matrix()),
        half.reshape(2 * 64, 64 * width),
        preferred_element_type=jnp.float32,
    ).astype(jnp.bfloat16)
    first = first.reshape(2, 64, 64, width).transpose(1, 0, 2, 3).reshape(64, 128, width)
    image = jnp.einsum(
        "lxm,lxy->lmy", first, jnp.asarray(tail_matrices()), preferred_element_type=jnp.float32
    )
    l_of = jnp.arange(64)[:, None, None] + 64 * jnp.arange(64)[None, None, :] - G // 2
    x = l_of.astype(jnp.float32) / G
    y = m_off[None, :, None].astype(jnp.float32) / G
    depth_term = jnp.sqrt(1.0 - y**2 - x**2)
    depth = (wa_index.astype(jnp.float32) - (wa_count - 1) / 2.0) * plane_step
    sc, ss = cos_sin_turns(depth * (depth_term - 1.0))
    screened = (image[:, :, :64] * sc - image[:, :, 64:] * ss) * (1.0 / G)
    share = 64 // wa_count
    if wa_count == 2:
        there = lax.dynamic_slice_in_dim(screened, (1 - wa_index) * share, share, 2)
        here = lax.dynamic_slice_in_dim(screened, wa_index * share, share, 2)
        came = lax.ppermute(
            there.transpose(1, 2, 0).reshape(width, -1).astype(jnp.bfloat16),
            "wa",
            [(0, 1), (1, 0)],
        )
        return here.transpose(1, 2, 0).reshape(width, -1) + came.astype(jnp.float32)
    parts = screened.transpose(1, 2, 0).reshape(width, G).astype(jnp.bfloat16)
    parts = parts.reshape(width, wa_count, G // wa_count)
    came = lax.all_to_all(parts, "wa", split_axis=1, concat_axis=1)
    return jnp.sum(came.astype(jnp.float32), axis=1)


def solution(mesh):
    in_specs = (
        P(("wa", "uv"), None, None),
        P(("wa", "uv"), None, None),
        P(("wa", "uv"), None),
        P(("wa", "uv")),
        P("wa", "uv"),
    )
    return jax.shard_map(
        on_device, mesh=mesh, in_specs=in_specs, out_specs=P("uv", "wa"), check_vma=False
    )
```

```python
import functools
import math

import jax
import jax.numpy as jnp
import ml_dtypes
import numpy as np
from jax import lax
from jax.experimental import pallas as pl
from jax.experimental.pallas import tpu as pltpu
from jax.sharding import PartitionSpec as P

G = 4096
SUB = 64
UNROLL = 4
plane_step = 6.0
full_turn = 2.0 * math.pi
BF = ml_dtypes.bfloat16


def turn_poly():
    nodes = np.cos(np.pi * (np.arange(256) + 0.5) / 256)
    z = (nodes + 1.0) / 8.0
    f = np.sqrt(z)
    cos_c = np.polynomial.chebyshev.cheb2poly(
        np.polynomial.chebyshev.chebfit(nodes, np.cos(2 * np.pi * f), 7)
    )
    sin_c = np.polynomial.chebyshev.cheb2poly(
        np.polynomial.chebyshev.chebfit(nodes, np.sin(2 * np.pi * f) / f, 7)
    )
    base = np.polynomial.Polynomial([-1.0, 8.0])
    out = []
    for coefs in (cos_c, sin_c):
        total = np.polynomial.Polynomial([0.0])
        for c in coefs[::-1]:
            total = total * base + c
        out.append([float(c) for c in total.coef])
    return out


COS_C, SIN_C = turn_poly()


def cos_sin_turns(turns):
    f = turns - jnp.round(turns)
    z = f * f
    c = jnp.full_like(z, COS_C[-1])
    for k in COS_C[-2::-1]:
        c = c * z + k
    s = jnp.full_like(z, SIN_C[-1])
    for k in SIN_C[-2::-1]:
        s = s * z + k
    return c, s * f


def factor_table():
    o = np.arange(SUB) - SUB // 2
    ang = full_turn / SUB * np.mod(o[:, None] * o[None, :], SUB)
    return np.cos(ang).astype(BF), (-np.sin(ang)).astype(BF)


def factor_matrix():
    fr, fi = factor_table()
    return np.block([[fr, -fi], [fi, fr]]).astype(BF)


def head_matrices():
    l0 = np.arange(64)[:, None]
    out = []
    for core in range(2):
        columns = []
        for source in range(2):
            t = (2 * np.arange(32) + (core ^ source))[None, :]
            ang = full_turn / 64 * np.mod(l0 * t, 64)
            c, s = np.cos(ang), np.sin(ang)
            columns.append(np.block([[c, -s], [s, c]]))
        out.append(np.concatenate(columns, axis=1))
    return np.stack(out).astype(BF)


def tail_matrices():
    l0 = np.arange(64)[:, None, None]
    p = np.arange(64)[None, :, None]
    l1 = np.arange(64)[None, None, :]
    ang = full_turn / G * np.mod(p * (l0 + 64 * l1), G)
    sign = 1.0 - 2.0 * ((p + l0) % 2)
    c, s = np.cos(ang) * sign, np.sin(ang) * sign
    top = np.concatenate([c, s], axis=2)
    bottom = np.concatenate([-s, c], axis=2)
    return np.concatenate([top, bottom], axis=1).astype(BF)


def gather_kernel(far, near, x_ref, out_ref, z_send, z_recv, y_send, y_recv, c_send, c_recv):
    me = lax.axis_index("uv")
    c = lax.rem(me, 2)
    b = lax.rem(me // 2, near)
    a = me // (2 * near)

    def at(da, db, dc):
        return (
            lax.rem(a + da + far, far) * near + lax.rem(b + db + near, near)
        ) * 2 + lax.rem(c + dc, 2)

    peers = [at(d, 0, 0) for d in range(1, far)]
    peers += [at(0, e, 0) for e in range(1, near)] + [at(0, 0, 1)]
    barrier = pltpu.get_barrier_semaphore()
    for peer in peers:
        pl.semaphore_signal(
            barrier, inc=1, device_id={"uv": peer}, device_id_type=pl.DeviceIdType.MESH
        )
    pl.semaphore_wait(barrier, len(peers))

    def copy(source, slot, target, send, recv):
        return pltpu.make_async_remote_copy(
            src_ref=source,
            dst_ref=out_ref.at[slot],
            send_sem=send,
            recv_sem=recv,
            device_id={"uv": target},
            device_id_type=pl.DeviceIdType.MESH,
        )

    sent = []

    def send(source, slot, target, send_sem, recv_sem):
        one = copy(source, slot, target, send_sem, recv_sem)
        one.start()
        sent.append(one)

    for d in range(1, far):
        send(x_ref, me, at(d, 0, 0), z_send.at[d], z_recv.at[d])
    for d in range(far):
        slot = at(-d, 0, 0)
        source = x_ref if d == 0 else out_ref.at[slot]
        if d > 0:
            copy(x_ref, slot, me, z_send.at[d], z_recv.at[d]).wait_recv()
        for e in range(1, near):
            k = d * near + e
            send(source, slot, at(0, e, 0), y_send.at[k], y_recv.at[k])
        k = d * near
        send(source, slot, at(0, 0, 1), c_send.at[k], c_recv.at[k])
        if d == 0:
            out_ref[me] = x_ref[...]
    for d in range(far):
        for e in range(1, near):
            k = d * near + e
            slot = at(-d, -e, 0)
            copy(x_ref, slot, me, y_send.at[k], y_recv.at[k]).wait_recv()
            send(out_ref.at[slot], slot, at(0, 0, 1), c_send.at[k], c_recv.at[k])
    for d in range(far):
        for e in range(near):
            k = d * near + e
            copy(x_ref, at(-d, -e, 1), me, c_send.at[k], c_recv.at[k]).wait_recv()
    for one in sent:
        one.wait_send()


def gather_all(packed, uv_count):
    chips = uv_count // 2
    near = 1 << ((chips.bit_length() - 1) // 2)
    far = chips // near
    sems = [far] * 2 + [far * near] * 4
    return pl.pallas_call(
        functools.partial(gather_kernel, far, near),
        out_shape=jax.ShapeDtypeStruct((uv_count,) + packed.shape, packed.dtype),
        in_specs=[pl.BlockSpec(memory_space=pltpu.VMEM)],
        out_specs=pl.BlockSpec(memory_space=pltpu.VMEM),
        scratch_shapes=[pltpu.SemaphoreType.DMA((n,)) for n in sems],
        compiler_params=pltpu.CompilerParams(
            collective_id=0, has_side_effects=True, vmem_limit_bytes=24 * 1024 * 1024
        ),
    )(packed)


def grid_kernel(
    width, blocks, tiles, counts, data_ref, cols_ref, moff_ref, mf_ref, d_ref,
    keep_ref, give_ref, acc, rows_f, phase, mine,
):
    j = pl.program_id(0)
    steps = pl.num_programs(0)

    @pl.when(j == 0)
    def _():
        acc[...] = jnp.zeros_like(acc)

    core = counts[steps]
    rows_f[...] = data_ref[0].astype(jnp.float32)
    for h in range(2):
        turn = jnp.bitwise_and((cols_ref[0] - G // 2) * moff_ref[h : h + 1, :], G - 1)
        pc, ps = cos_sin_turns(turn.astype(jnp.float32) * (1.0 / G))
        phase[2 * h] = pc
        phase[2 * h + 1] = ps

    def pick(i, n):
        mine[n] = i
        return n + jnp.where(lax.rem(tiles[j * blocks + i], 2) == core, 1, 0)

    total = lax.fori_loop(0, counts[j], pick, 0)
    k_len = data_ref.shape[2]
    offs = lax.broadcasted_iota(jnp.int32, (8, k_len), 0).astype(jnp.float32)
    fine = offs * (1.0 / SUB)
    coarse = (offs - 4.0) * (8.0 / SUB)
    scale = 1.0 / math.sqrt(k_len)

    def expand(pr, pi, c1, s1):
        res, ims = [], []
        for a in range(8):
            ar, ai = pr[a : a + 1, :], pi[a : a + 1, :]
            res.append(ar * c1 - ai * s1)
            ims.append(ar * s1 + ai * c1)
        return jnp.concatenate(res + ims, axis=0).astype(jnp.bfloat16)

    def step(it, carry):
        lefts, rights, index = [], [], []
        for k in range(UNROLL):
            n = it * UNROLL + k
            i = jnp.where(n < total, mine[n], 0)
            index.append(i)
            keep = jnp.where(n < total, scale, 0.0)
            vr, vi, u, v = (rows_f[pl.ds(q * blocks + i, 1), :] for q in range(4))
            c1, s1 = cos_sin_turns(fine * u)
            c8, s8 = cos_sin_turns(coarse * u)
            lefts.append(
                expand((vr * c8 - vi * s8) * keep, (vr * s8 + vi * c8) * keep, c1, s1)
            )
            d1, t1 = cos_sin_turns(fine * v)
            d8, t8 = cos_sin_turns(coarse * v)
            rights.append(expand(d8, t8, d1, t1))
        parts = []
        for k in range(UNROLL):
            s = lax.dot_general(
                lefts[k], rights[k], (((1,), (1,)), ((), ())), preferred_element_type=jnp.float32
            ).astype(jnp.bfloat16)
            c = jnp.dot(mf_ref[...], s, preferred_element_type=jnp.float32).astype(jnp.bfloat16)
            parts.append(jnp.concatenate([c[:SUB], c[SUB:]], axis=1))
        joined = jnp.concatenate(parts, axis=0)
        for h in range(2):
            out = jnp.dot(
                joined,
                d_ref[:, 2 * h * width : 2 * (h + 1) * width],
                preferred_element_type=jnp.float32,
            )
            for k in range(UNROLL):
                i = index[k]
                pr = phase[2 * h, pl.ds(i, 1), :]
                pi = phase[2 * h + 1, pl.ds(i, 1), :]
                hr = out[k * SUB : (k + 1) * SUB, :width]
                hi = out[k * SUB : (k + 1) * SUB, width:]
                rows = pl.ds(pl.multiple_of(tiles[j * blocks + i] // 2 * SUB, SUB), SUB)
                acc[2 * h, rows, :] += hr * pr - hi * pi
                acc[2 * h + 1, rows, :] += hr * pi + hi * pr
        return carry

    lax.fori_loop(0, (total + UNROLL - 1) // UNROLL, step, 0)

    @pl.when(j == steps - 1)
    def _():
        half_rows = acc.shape[1] // SUB
        for h, ref in enumerate((keep_ref, give_ref)):
            for c in range(2):
                ref[c] = acc[2 * h + c].astype(jnp.bfloat16).reshape(half_rows, SUB, width)


def on_device(visibility, coords, tile_row, col_offset, live_count):
    uv_count = lax.axis_size("uv")
    wa_count = lax.axis_size("wa")
    uv_index = lax.axis_index("uv")
    wa_index = lax.axis_index("wa")
    blocks = visibility.shape[0]
    k_len = visibility.shape[2]
    width = G // uv_count
    core = jnp.mod(uv_index, 2)
    numbers = jnp.stack(
        [
            tile_row[:, 0],
            col_offset // SUB,
            jnp.mod(col_offset, SUB),
            jnp.broadcast_to(live_count[0], (blocks,)),
        ]
    )
    numbers = jnp.pad(numbers, ((0, 12), (0, k_len - blocks))).astype(jnp.bfloat16)
    packed = jnp.concatenate(
        [visibility[:, 0], visibility[:, 1], coords[:, 0], coords[:, 1], numbers], axis=0
    )
    all_data = gather_all(packed, uv_count)
    came_numbers = all_data[:, 4 * blocks : 4 * blocks + 4, :blocks].astype(jnp.int32)
    tiles = came_numbers[:, 0].reshape(-1)
    cols = (came_numbers[:, 1] * SUB + came_numbers[:, 2])[:, :, None]
    counts = jnp.concatenate([came_numbers[:, 3, 0], core[None]])

    m_off = uv_index * width + jnp.arange(width) - G // 2
    partner = uv_index + 1 - 2 * core
    m_both = jnp.stack([m_off, partner * width + jnp.arange(width) - G // 2])

    fr, fi = factor_table()
    fr, fi = fr.astype(np.float32), fi.astype(np.float32)
    qt = jnp.mod(jnp.arange(SUB)[:, None] * m_both.reshape(-1)[None, :], G).astype(jnp.float32)
    qc, qs = cos_sin_turns(qt * (1.0 / G))
    both = jnp.dot(
        jnp.asarray(np.block([[fr.T, -fi.T], [fi.T, fr.T]]) / SUB),
        jnp.concatenate([qc, qs], axis=0),
        precision=lax.Precision.HIGHEST,
    )
    dr, di = both[:SUB].reshape(SUB, 2, width), both[SUB:].reshape(SUB, 2, width)
    ddr = jnp.concatenate([dr, -di], axis=0)
    ddi = jnp.concatenate([di, dr], axis=0)
    d_table = jnp.concatenate(
        [jnp.stack([ddr, ddi], axis=2), jnp.stack([-ddi, ddr], axis=2)], axis=0
    ).reshape(4 * SUB, 4 * width).astype(jnp.bfloat16)

    rows = packed.shape[0]
    half_tiles = G // SUB // 2
    shape = (2, half_tiles, SUB, width)
    spec = pltpu.PrefetchScalarGridSpec(
        num_scalar_prefetch=2,
        grid=(uv_count,),
        in_specs=[
            pl.BlockSpec((1, rows, k_len), lambda j, *_: (j, 0, 0)),
            pl.BlockSpec((1, blocks, 1), lambda j, *_: (j, 0, 0)),
            pl.BlockSpec((2, width), lambda j, *_: (0, 0)),
            pl.BlockSpec((2 * SUB, 2 * SUB), lambda j, *_: (0, 0)),
            pl.BlockSpec((4 * SUB, 4 * width), lambda j, *_: (0, 0)),
        ],
        out_specs=[pl.BlockSpec(shape, lambda j, *_: (0, 0, 0, 0))] * 2,
        scratch_shapes=[
            pltpu.VMEM((4, G // 2, width), jnp.float32),
            pltpu.VMEM((rows, k_len), jnp.float32),
            pltpu.VMEM((4, blocks, width), jnp.float32),
            pltpu.SMEM((blocks + UNROLL,), jnp.int32),
        ],
    )
    own, give = pl.pallas_call(
        functools.partial(grid_kernel, width, blocks),
        out_shape=[jax.ShapeDtypeStruct(shape, jnp.bfloat16)] * 2,
        grid_spec=spec,
        compiler_params=pltpu.CompilerParams(vmem_limit_bytes=40 * 1024 * 1024),
    )(tiles, counts, all_data, cols, m_both, jnp.asarray(factor_matrix()), d_table)
    came_half = lax.ppermute(give, "uv", [(n, n ^ 1) for n in range(uv_count)])
    half = jnp.concatenate([own, came_half], axis=0)

    first = jnp.dot(
        jnp.asarray(head_matrices())[core],
        half.reshape(2 * 64, 64 * width),
        preferred_element_type=jnp.float32,
    ).astype(jnp.bfloat16)
    first = first.reshape(2, 64, 64, width).transpose(1, 0, 2, 3).reshape(64, 128, width)
    image = jnp.einsum(
        "lxm,lxy->lmy", first, jnp.asarray(tail_matrices()), preferred_element_type=jnp.float32
    )
    l_of = jnp.arange(64)[:, None, None] + 64 * jnp.arange(64)[None, None, :] - G // 2
    x = l_of.astype(jnp.float32) / G
    y = m_off[None, :, None].astype(jnp.float32) / G
    depth_term = jnp.sqrt(1.0 - y**2 - x**2)
    depth = (wa_index.astype(jnp.float32) - (wa_count - 1) / 2.0) * plane_step
    sc, ss = cos_sin_turns(depth * (depth_term - 1.0))
    screened = (image[:, :, :64] * sc - image[:, :, 64:] * ss) * (1.0 / G)
    share = 64 // wa_count
    if wa_count == 2:
        there = lax.dynamic_slice_in_dim(screened, (1 - wa_index) * share, share, 2)
        here = lax.dynamic_slice_in_dim(screened, wa_index * share, share, 2)
        came = lax.ppermute(
            there.transpose(1, 2, 0).reshape(width, -1).astype(jnp.bfloat16),
            "wa",
            [(0, 1), (1, 0)],
        )
        return here.transpose(1, 2, 0).reshape(width, -1) + came.astype(jnp.float32)
    parts = screened.transpose(1, 2, 0).reshape(width, G).astype(jnp.bfloat16)
    parts = parts.reshape(width, wa_count, G // wa_count)
    came = lax.all_to_all(parts, "wa", split_axis=1, concat_axis=1)
    return jnp.sum(came.astype(jnp.float32), axis=1)


def solution(mesh):
    in_specs = (
        P(("wa", "uv"), None, None),
        P(("wa", "uv"), None, None),
        P(("wa", "uv"), None),
        P(("wa", "uv")),
        P("wa", "uv"),
    )
    return jax.shard_map(
        on_device, mesh=mesh, in_specs=in_specs, out_specs=P("uv", "wa"), check_vma=False
    )
```

```python
import functools
import math

import jax
import jax.numpy as jnp
import ml_dtypes
import numpy as np
from jax import lax
from jax.experimental import pallas as pl
from jax.experimental.pallas import tpu as pltpu
from jax.sharding import PartitionSpec as P

G = 4096
SUB = 64
UNROLL = 8
plane_step = 6.0
full_turn = 2.0 * math.pi
BF = ml_dtypes.bfloat16


def turn_poly():
    nodes = np.cos(np.pi * (np.arange(256) + 0.5) / 256)
    z = (nodes + 1.0) / 8.0
    f = np.sqrt(z)
    cos_c = np.polynomial.chebyshev.cheb2poly(
        np.polynomial.chebyshev.chebfit(nodes, np.cos(2 * np.pi * f), 7)
    )
    sin_c = np.polynomial.chebyshev.cheb2poly(
        np.polynomial.chebyshev.chebfit(nodes, np.sin(2 * np.pi * f) / f, 7)
    )
    base = np.polynomial.Polynomial([-1.0, 8.0])
    out = []
    for coefs in (cos_c, sin_c):
        total = np.polynomial.Polynomial([0.0])
        for c in coefs[::-1]:
            total = total * base + c
        out.append([float(c) for c in total.coef])
    return out


COS_C, SIN_C = turn_poly()


def cos_sin_turns(turns):
    f = turns - jnp.round(turns)
    z = f * f
    c = jnp.full_like(z, COS_C[-1])
    for k in COS_C[-2::-1]:
        c = c * z + k
    s = jnp.full_like(z, SIN_C[-1])
    for k in SIN_C[-2::-1]:
        s = s * z + k
    return c, s * f


def factor_table():
    o = np.arange(SUB) - SUB // 2
    ang = full_turn / SUB * np.mod(o[:, None] * o[None, :], SUB)
    return np.cos(ang).astype(BF), (-np.sin(ang)).astype(BF)


def factor_matrix():
    fr, fi = factor_table()
    return np.block([[fr, -fi], [fi, fr]]).astype(BF)


def head_matrices():
    l0 = np.arange(64)[:, None]
    out = []
    for core in range(2):
        columns = []
        for source in range(2):
            t = (2 * np.arange(32) + (core ^ source))[None, :]
            ang = full_turn / 64 * np.mod(l0 * t, 64)
            c, s = np.cos(ang), np.sin(ang)
            columns.append(np.block([[c, -s], [s, c]]))
        out.append(np.concatenate(columns, axis=1))
    return np.stack(out).astype(BF)


def tail_matrices():
    l0 = np.arange(64)[:, None, None]
    p = np.arange(64)[None, :, None]
    l1 = np.arange(64)[None, None, :]
    ang = full_turn / G * np.mod(p * (l0 + 64 * l1), G)
    sign = 1.0 - 2.0 * ((p + l0) % 2)
    c, s = np.cos(ang) * sign, np.sin(ang) * sign
    top = np.concatenate([c, s], axis=2)
    bottom = np.concatenate([-s, c], axis=2)
    return np.concatenate([top, bottom], axis=1).astype(BF)


def split_tail(parts):
    whole = tail_matrices().reshape(64, 128, 2, parts, 64 // parts)
    return np.ascontiguousarray(whole.transpose(3, 0, 1, 2, 4)).reshape(parts, 64, 128, -1)


def gather_kernel(far, near, x_ref, out_ref, z_send, z_recv, y_send, y_recv, c_send, c_recv):
    me = lax.axis_index("uv")
    c = lax.rem(me, 2)
    b = lax.rem(me // 2, near)
    a = me // (2 * near)

    def at(da, db, dc):
        return (
            lax.rem(a + da + far, far) * near + lax.rem(b + db + near, near)
        ) * 2 + lax.rem(c + dc, 2)

    peers = [at(d, 0, 0) for d in range(1, far)]
    peers += [at(0, e, 0) for e in range(1, near)] + [at(0, 0, 1)]
    barrier = pltpu.get_barrier_semaphore()
    for peer in peers:
        pl.semaphore_signal(
            barrier, inc=1, device_id={"uv": peer}, device_id_type=pl.DeviceIdType.MESH
        )
    pl.semaphore_wait(barrier, len(peers))

    def copy(source, slot, target, send, recv):
        return pltpu.make_async_remote_copy(
            src_ref=source,
            dst_ref=out_ref.at[slot],
            send_sem=send,
            recv_sem=recv,
            device_id={"uv": target},
            device_id_type=pl.DeviceIdType.MESH,
        )

    sent = []

    def send(source, slot, target, send_sem, recv_sem):
        one = copy(source, slot, target, send_sem, recv_sem)
        one.start()
        sent.append(one)

    for d in range(1, far):
        send(x_ref, me, at(d, 0, 0), z_send.at[d], z_recv.at[d])
    for d in range(far):
        slot = at(-d, 0, 0)
        source = x_ref if d == 0 else out_ref.at[slot]
        if d > 0:
            copy(x_ref, slot, me, z_send.at[d], z_recv.at[d]).wait_recv()
        for e in range(1, near):
            k = d * near + e
            send(source, slot, at(0, e, 0), y_send.at[k], y_recv.at[k])
        k = d * near
        send(source, slot, at(0, 0, 1), c_send.at[k], c_recv.at[k])
        if d == 0:
            out_ref[me] = x_ref[...]
    for d in range(far):
        for e in range(1, near):
            k = d * near + e
            slot = at(-d, -e, 0)
            copy(x_ref, slot, me, y_send.at[k], y_recv.at[k]).wait_recv()
            send(out_ref.at[slot], slot, at(0, 0, 1), c_send.at[k], c_recv.at[k])
    for d in range(far):
        for e in range(near):
            k = d * near + e
            copy(x_ref, at(-d, -e, 1), me, c_send.at[k], c_recv.at[k]).wait_recv()
    for one in sent:
        one.wait_send()


def gather_all(packed, uv_count):
    chips = uv_count // 2
    near = 1 << ((chips.bit_length() - 1) // 2)
    far = chips // near
    sems = [far] * 2 + [far * near] * 4
    return pl.pallas_call(
        functools.partial(gather_kernel, far, near),
        out_shape=jax.ShapeDtypeStruct((uv_count,) + packed.shape, packed.dtype),
        in_specs=[pl.BlockSpec(memory_space=pltpu.VMEM)],
        out_specs=pl.BlockSpec(memory_space=pltpu.VMEM),
        scratch_shapes=[pltpu.SemaphoreType.DMA((n,)) for n in sems],
        compiler_params=pltpu.CompilerParams(
            collective_id=0, has_side_effects=True, vmem_limit_bytes=24 * 1024 * 1024
        ),
    )(packed)


def grid_kernel(
    width, blocks, tiles, counts, data_ref, cols_ref, moff_ref, mf_ref, d_ref,
    keep_ref, give_ref, acc, rows_f, phase, mine,
):
    devices = data_ref.shape[0]
    acc[...] = jnp.zeros_like(acc)
    core = counts[devices]

    def spread(j, found):
        rows_f[j] = data_ref[j].astype(jnp.float32)
        for h in range(2):
            turn = jnp.bitwise_and((cols_ref[j] - G // 2) * moff_ref[h : h + 1, :], G - 1)
            pc, ps = cos_sin_turns(turn.astype(jnp.float32) * (1.0 / G))
            phase[j, 2 * h] = pc
            phase[j, 2 * h + 1] = ps

        def pick(i, n):
            mine[n] = j * blocks + i
            return n + jnp.where(lax.rem(tiles[j * blocks + i], 2) == core, 1, 0)

        return lax.fori_loop(0, counts[j], pick, found)

    total = lax.fori_loop(0, devices, spread, 0)
    k_len = data_ref.shape[2]
    offs = lax.broadcasted_iota(jnp.int32, (8, k_len), 0).astype(jnp.float32)
    fine = offs * (1.0 / SUB)
    coarse = (offs - 4.0) * (8.0 / SUB)
    scale = 1.0 / math.sqrt(k_len)

    def expand(pr, pi, c1, s1):
        res, ims = [], []
        for a in range(8):
            ar, ai = pr[a : a + 1, :], pi[a : a + 1, :]
            res.append(ar * c1 - ai * s1)
            ims.append(ar * s1 + ai * c1)
        return jnp.concatenate(res + ims, axis=0).astype(jnp.bfloat16)

    def step(it, carry):
        lefts, rights, index = [], [], []
        for k in range(UNROLL):
            n = it * UNROLL + k
            g = jnp.where(n < total, mine[n], 0)
            j = g // blocks
            i = g - j * blocks
            index.append((g, j, i))
            keep = jnp.where(n < total, scale, 0.0)
            vr, vi, u, v = (rows_f[j, pl.ds(q * blocks + i, 1), :] for q in range(4))
            c1, s1 = cos_sin_turns(fine * u)
            c8, s8 = cos_sin_turns(coarse * u)
            lefts.append(
                expand((vr * c8 - vi * s8) * keep, (vr * s8 + vi * c8) * keep, c1, s1)
            )
            d1, t1 = cos_sin_turns(fine * v)
            d8, t8 = cos_sin_turns(coarse * v)
            rights.append(expand(d8, t8, d1, t1))
        parts = []
        for k in range(UNROLL):
            s = lax.dot_general(
                lefts[k], rights[k], (((1,), (1,)), ((), ())), preferred_element_type=jnp.float32
            ).astype(jnp.bfloat16)
            c = jnp.dot(mf_ref[...], s, preferred_element_type=jnp.float32).astype(jnp.bfloat16)
            parts.append(jnp.concatenate([c[:SUB], c[SUB:]], axis=1))
        joined = jnp.concatenate(parts, axis=0)
        for h in range(2):
            out = jnp.dot(
                joined,
                d_ref[:, 2 * h * width : 2 * (h + 1) * width],
                preferred_element_type=jnp.float32,
            )
            for k in range(UNROLL):
                g, j, i = index[k]
                pr = phase[j, 2 * h, pl.ds(i, 1), :]
                pi = phase[j, 2 * h + 1, pl.ds(i, 1), :]
                hr = out[k * SUB : (k + 1) * SUB, :width]
                hi = out[k * SUB : (k + 1) * SUB, width:]
                rows = pl.ds(pl.multiple_of(tiles[g] // 2 * SUB, SUB), SUB)
                acc[2 * h, rows, :] += hr * pr - hi * pi
                acc[2 * h + 1, rows, :] += hr * pi + hi * pr
        return carry

    lax.fori_loop(0, (total + UNROLL - 1) // UNROLL, step, 0)

    half_rows = acc.shape[1] // SUB
    for h, ref in enumerate((keep_ref, give_ref)):
        for c in range(2):
            ref[c] = acc[2 * h + c].astype(jnp.bfloat16).reshape(half_rows, SUB, width)


def on_device(visibility, coords, tile_row, col_offset, live_count):
    uv_count = lax.axis_size("uv")
    wa_count = lax.axis_size("wa")
    uv_index = lax.axis_index("uv")
    wa_index = lax.axis_index("wa")
    blocks = visibility.shape[0]
    k_len = visibility.shape[2]
    width = G // uv_count
    core = jnp.mod(uv_index, 2)
    numbers = jnp.stack(
        [
            tile_row[:, 0],
            col_offset // SUB,
            jnp.mod(col_offset, SUB),
            jnp.broadcast_to(live_count[0], (blocks,)),
        ]
    )
    numbers = jnp.pad(numbers, ((0, 12), (0, k_len - blocks))).astype(jnp.bfloat16)
    packed = jnp.concatenate(
        [visibility[:, 0], visibility[:, 1], coords[:, 0], coords[:, 1], numbers], axis=0
    )
    all_data = gather_all(packed, uv_count)
    came_numbers = all_data[:, 4 * blocks : 4 * blocks + 4, :blocks].astype(jnp.int32)
    tiles = came_numbers[:, 0].reshape(-1)
    cols = (came_numbers[:, 1] * SUB + came_numbers[:, 2])[:, :, None]
    counts = jnp.concatenate([came_numbers[:, 3, 0], core[None]])

    m_off = uv_index * width + jnp.arange(width) - G // 2
    partner = uv_index + 1 - 2 * core
    m_both = jnp.stack([m_off, partner * width + jnp.arange(width) - G // 2])

    fr, fi = factor_table()
    fr, fi = fr.astype(np.float32), fi.astype(np.float32)
    qt = jnp.mod(jnp.arange(SUB)[:, None] * m_both.reshape(-1)[None, :], G).astype(jnp.float32)
    qc, qs = cos_sin_turns(qt * (1.0 / G))
    both = jnp.dot(
        jnp.asarray(np.block([[fr.T, -fi.T], [fi.T, fr.T]]) / SUB),
        jnp.concatenate([qc, qs], axis=0),
        precision=lax.Precision.HIGHEST,
    )
    dr, di = both[:SUB].reshape(SUB, 2, width), both[SUB:].reshape(SUB, 2, width)
    ddr = jnp.concatenate([dr, -di], axis=0)
    ddi = jnp.concatenate([di, dr], axis=0)
    d_table = jnp.concatenate(
        [jnp.stack([ddr, ddi], axis=2), jnp.stack([-ddi, ddr], axis=2)], axis=0
    ).reshape(4 * SUB, 4 * width).astype(jnp.bfloat16)

    rows = packed.shape[0]
    half_tiles = G // SUB // 2
    shape = (2, half_tiles, SUB, width)
    vmem = pl.BlockSpec(memory_space=pltpu.VMEM)
    smem = pl.BlockSpec(memory_space=pltpu.SMEM)
    own, give = pl.pallas_call(
        functools.partial(grid_kernel, width, blocks),
        out_shape=[jax.ShapeDtypeStruct(shape, jnp.bfloat16)] * 2,
        in_specs=[smem, smem, vmem, vmem, vmem, vmem, vmem],
        out_specs=[vmem, vmem],
        scratch_shapes=[
            pltpu.VMEM((4, G // 2, width), jnp.float32),
            pltpu.VMEM((uv_count, rows, k_len), jnp.float32),
            pltpu.VMEM((uv_count, 4, blocks, width), jnp.float32),
            pltpu.SMEM((uv_count * blocks + UNROLL,), jnp.int32),
        ],
        compiler_params=pltpu.CompilerParams(vmem_limit_bytes=48 * 1024 * 1024),
    )(tiles, counts, all_data, cols, m_both, jnp.asarray(factor_matrix()), d_table)
    came_half = lax.ppermute(give, "uv", [(n, n ^ 1) for n in range(uv_count)])
    half = jnp.concatenate([own, came_half], axis=0)

    first = jnp.dot(
        jnp.asarray(head_matrices())[core],
        half.reshape(2 * 64, 64 * width),
        preferred_element_type=jnp.float32,
    ).astype(jnp.bfloat16)
    first = first.reshape(2, 64, 64, width).transpose(1, 0, 2, 3).reshape(64, 128, width)
    share = 64 // wa_count
    depth = (wa_index.astype(jnp.float32) - (wa_count - 1) / 2.0) * plane_step
    y = m_off[None, :, None].astype(jnp.float32) / G
    tail = jnp.asarray(split_tail(wa_count))

    def shares_of(part):
        image = jnp.einsum("lxm,lxy->lmy", first, tail[part], preferred_element_type=jnp.float32)
        l1 = part * share + jnp.arange(share)[None, None, :]
        x = (jnp.arange(64)[:, None, None] + 64 * l1 - G // 2).astype(jnp.float32) / G
        depth_term = jnp.sqrt(1.0 - y**2 - x**2)
        sc, ss = cos_sin_turns(depth * (depth_term - 1.0))
        screened = (image[:, :, :share] * sc - image[:, :, share:] * ss) * (1.0 / G)
        return screened

    def in_order(screened):
        return screened.transpose(1, 2, 0).reshape(width, G // wa_count)

    if wa_count == 2:
        away = in_order(shares_of(1 - wa_index).astype(jnp.bfloat16))
        came = lax.ppermute(away, "wa", [(0, 1), (1, 0)])
        return in_order(shares_of(wa_index)) + came.astype(jnp.float32)
    parts = jnp.stack(
        [in_order(shares_of(part).astype(jnp.bfloat16)) for part in range(wa_count)], axis=1
    )
    came = lax.all_to_all(parts, "wa", split_axis=1, concat_axis=1)
    return jnp.sum(came.astype(jnp.float32), axis=1)


def solution(mesh):
    in_specs = (
        P(("wa", "uv"), None, None),
        P(("wa", "uv"), None, None),
        P(("wa", "uv"), None),
        P(("wa", "uv")),
        P("wa", "uv"),
    )
    return jax.shard_map(
        on_device, mesh=mesh, in_specs=in_specs, out_specs=P("uv", "wa"), check_vma=False
    )
```
